32 devices in a mesh: fsdp: 8 (over y, x, core), tensor: 4 (over z).
Axes of the slice: x: 2, y: 2, z: 4, core: 2. Of those that a mesh axis runs over, the one named last changes fastest.
Arguments:
- saved_weight: float32 [7168, 8192], P(('fsdp', 'tensor')), may hold values from -6 to 6
- saved_first: float32 [7168, 8192], P(('fsdp', 'tensor')), may hold values from -3 to 3
- saved_second: float32 [7168, 8192], P(('fsdp', 'tensor')), may hold values from 0.1 to 2
- saved_order: int32 [7168], P(('fsdp', 'tensor')), may hold values from 0 to 223, as said below
- mask: int32 [7168, 8192], P('tensor', 'fsdp'), may hold values 0 or 1
- hidden: bfloat16 [2048, 7168], P('fsdp', 'tensor'), may hold values from -6 to 6
- cotangent: bfloat16 [2048, 8192], P('fsdp'), may hold values from -6 to 6
Outputs:
- output: bfloat16 [2048, 8192], P('fsdp', 'tensor')
- hidden_grad: bfloat16 [2048, 7168], P('fsdp', 'tensor')
- new_weight: float32 [7168, 8192], P('tensor', 'fsdp')
- new_first: float32 [7168, 8192], P('tensor', 'fsdp')
- new_second: float32 [7168, 8192], P('tensor', 'fsdp')
The draws below stay inside these ranges and needn't reach their ends.
Inputs may be any that keep to these rules, and one draw needn't show every extreme that they name: `saved_order`: each aligned block of 224 entries holds every number of 0 to 223 once.
All inputs are finite; a program needn't handle non-finite values. No bound on the sum of `mask` on one device may be relied on, other than what follows from the above.
Results may differ from the reference program's by a relative error of at most 0.005.
Values may be sent and summed in bfloat16 or wider, within the bound.
A program may use at most 192 MiB of HBM per device.

```python
import math
import jax
import jax.numpy as jnp
from jax import lax

D = 8192
R = 7168
STEP = 1000
TOK_DEV = 256
TOKENS = 2048
BAND = 224
N_FSDP = 8


def draw_saved_order(key, part):
    base_rows = jnp.tile(jnp.arange(BAND, dtype=jnp.int32), (R // BAND, 1))
    shuffled = jax.random.permutation(jax.random.fold_in(key, 17), base_rows, axis=1, independent=True)
    return shuffled.reshape(-1).astype(jnp.int32)


def touch_ends(result, rng, smallest, largest):
    place = [jax.random.randint(jax.random.fold_in(rng, axis), (), 0, length) for axis, length in enumerate(result.shape)]
    main_axis = result.shape.index(max(result.shape))
    next_to = place[:main_axis] + [(place[main_axis] + 1) % result.shape[main_axis]] + place[main_axis + 1:]
    return result.at[tuple(place)].set(smallest).at[tuple(next_to)].set(largest)


def raised(values, stream_key, source, target, parts, factor):
    owner, partner = [(jnp.arange(values.shape[position]) // (values.shape[position] // parts)).reshape([-1 if axis == position else 1 for axis in range(values.ndim)]) for position in (source, target)]
    chosen = jax.random.permutation(stream_key, parts)[partner]
    strong = (owner == chosen) | (owner == (partner + parts // 2) % parts)
    return jnp.where(strong, factor * values, values)


def level_of(rng, extent, cuts, low, high):
    level = 1.0
    for axis_at, parts in cuts:
        draws = jax.random.uniform(jax.random.fold_in(jax.random.fold_in(rng, 6), axis_at), (parts,), jnp.float32, low / len(cuts), high / len(cuts))
        level = level * jnp.repeat(jnp.exp(draws), extent[axis_at] // parts).reshape((-1,) + (1,) * (len(extent) - 1 - axis_at))
    return level


def bell_draw(rng, shape, scale, bound, split=(), kind=jnp.bfloat16):
    entries = scale * jax.random.normal(rng, shape, jnp.float32)
    if split:
        entries = entries * level_of(rng, shape, split, -0.22, 0.18)
    return jnp.clip(entries, -bound, bound).astype(kind)


def heavy_noise(stream_key, dims, scale, most, shards, heavy, kind=jnp.bfloat16):
    entries = scale * jax.random.normal(stream_key, dims, jnp.float32)
    if shards:
        entries = entries * level_of(stream_key, dims, shards, -0.22, 0.18)
    return jnp.clip(raised(entries, jax.random.fold_in(stream_key, 3), *heavy), -most, most).astype(kind)


def setup_inputs(seed: int = 0) -> dict:
    key_of = jax.random.split(jax.random.key(seed), 8)
    return {
        "saved_weight": bell_draw(key_of[0], (R, D), 1.0, 6.0, ((0, 32),), jnp.float32),
        "saved_first": bell_draw(key_of[1], (R, D), 0.5, 3.0, ((0, 32),), jnp.float32),
        "saved_second": jnp.clip(jnp.exp(math.log(2.0) - 2.9957323 * jax.random.uniform(key_of[2], (R, D), jnp.float32) ** level_of(key_of[2], (R, D), ((0, 32),), -0.2, 0.2)), 0.1, 2.0),
        "saved_order": draw_saved_order(jax.random.fold_in(key_of[7], 71), 0),
        "mask": touch_ends((jax.random.randint(key_of[4], (R, D), 0, 2) < 1).astype(jnp.int32), jax.random.fold_in(key_of[4], 1), 0, 1),
        "hidden": bell_draw(key_of[5], (TOKENS, R), 1.0, 6.0, ((0, 8), (1, 4))),
        "cotangent": heavy_noise(key_of[6], (TOKENS, D), 1.0, 6.0, ((0, 8),), (0, 1, 8, 2.0)),
    }


beta_first = 0.9
beta_second = 0.999
learn_rate = 0.01
decay_rate = 0.1
epsilon = 1e-08

def reference(saved_weight, saved_first, saved_second, saved_order, mask, hidden, cotangent):
    ordered = saved_order.reshape(-1, BAND)
    offsets = (jnp.arange(ordered.shape[0], dtype=jnp.int32) * BAND)[:, None]
    inverse = (jnp.argsort(ordered, axis=1).astype(jnp.int32) + offsets).reshape(-1)
    weight = jnp.take(saved_weight, inverse, axis=0)
    first = jnp.take(saved_first, inverse, axis=0)
    second = jnp.take(saved_second, inverse, axis=0)
    keep = mask.astype(jnp.float32)
    masked = (weight * keep).astype(jnp.bfloat16)
    scale_alpha = R ** (-0.5)
    output = (scale_alpha * jnp.dot(hidden, masked, preferred_element_type=jnp.float32)).astype(jnp.bfloat16)
    hidden_grad = (scale_alpha * lax.dot_general(cotangent, masked, (((1,), (1,)), ((), ())), preferred_element_type=jnp.float32)).astype(jnp.bfloat16)
    hidden_blocks = hidden.reshape(N_FSDP, TOK_DEV, R)
    cot_blocks = cotangent.reshape(N_FSDP, TOK_DEV, D)

    def accumulate(carry, pair):
        hid_block, cot_block = pair
        partial_sum = lax.dot_general(hid_block, cot_block, (((0,), (0,)), ((), ())), preferred_element_type=jnp.float32)
        rounded = (scale_alpha * partial_sum).astype(jnp.bfloat16)
        return (carry + rounded.astype(jnp.float32), None)
    summed, unused = lax.scan(accumulate, jnp.zeros((R, D), jnp.float32), (hidden_blocks, cot_blocks))
    grad = keep * summed
    new_first = beta_first * first + (1.0 - beta_first) * grad
    new_second = beta_second * second + (1.0 - beta_second) * grad * grad
    corr_first = 1.0 - beta_first ** (STEP + 1)
    corr_second = 1.0 - beta_second ** (STEP + 1)
    update = new_first / corr_first / (jnp.sqrt(new_second / corr_second) + epsilon)
    new_weight = keep * (weight - learn_rate * (update + decay_rate * weight))
    return (output, hidden_grad, new_weight, new_first, new_second)
```

```python
import functools

import jax
import jax.numpy as jnp
from jax import lax
from jax.experimental import pallas as pl
from jax.experimental.pallas import tpu as pltpu
from jax.sharding import PartitionSpec as P

STEP = 1000


beta_first = 0.9
beta_second = 0.999
learn_rate = 0.01
decay_rate = 0.1
epsilon = 1e-08

MESH = pl.DeviceIdType.MESH
ANY = pl.BlockSpec(memory_space=pl.ANY)


def greet(nf, nt):
    f, t = lax.axis_index("fsdp"), lax.axis_index("tensor")
    barrier = pltpu.get_barrier_semaphore()
    for k in range(1, nf):
        pl.semaphore_signal(barrier, inc=1, device_id=(lax.rem(f + k, nf), t), device_id_type=MESH)
    for j in range(1, nt):
        pl.semaphore_signal(barrier, inc=1, device_id=(f, lax.rem(t + j, nt)), device_id_type=MESH)
    pl.semaphore_wait(barrier, nf - 1 + nt - 1)


class Spread:
    def __init__(self, nf, nt, block_of, stage, send, recv):
        self.nf, self.nt, self.block_of, self.stage, self.send, self.recv = nf, nt, block_of, stage, send, recv
        self.f, self.t = lax.axis_index("fsdp"), lax.axis_index("tensor")
        self.sent = []

    def start(self):
        f, t, nf = self.f, self.t, self.nf
        for k in list(range(2, nf)) + [1]:
            to = lax.rem(f + k, nf)
            copy = pltpu.make_async_remote_copy(
                src_ref=self.block_of(to), dst_ref=self.stage.at[f],
                send_sem=self.send.at[k], recv_sem=self.recv.at[k],
                device_id=(to, t), device_id_type=MESH,
            )
            copy.start()
            self.sent.append(copy)
        pltpu.make_async_copy(self.block_of(f), self.stage.at[f], self.recv.at[0]).start()

    def wait_for(self, owner):
        k = lax.rem(self.f - owner + self.nf, self.nf)
        slot = self.stage.at[owner]
        pltpu.make_async_copy(slot, slot, self.recv.at[k]).wait()

    def finish(self):
        for copy in self.sent:
            copy.wait_send()


class Along:
    def __init__(self, nf, nt, stage, out, send, recv, local):
        self.nf, self.nt, self.stage, self.out = nf, nt, stage, out
        self.send, self.recv, self.local = send, recv, local
        self.f, self.t = lax.axis_index("fsdp"), lax.axis_index("tensor")
        self.g = nf // nt
        self.sent, self.kept = [], []

    def start(self, ready):
        f, t, nt, g = self.f, self.t, self.nt, self.g
        for j in list(range(1, nt)) + [0]:
            to = lax.rem(t + j, nt)
            for i in range(g):
                owner = to * g + i
                if ready is not None:
                    ready(owner)
                if j:
                    copy = pltpu.make_async_remote_copy(
                        src_ref=self.stage.at[owner], dst_ref=self.out.at[i, t],
                        send_sem=self.send.at[j, i], recv_sem=self.recv.at[j, i],
                        device_id=(f, to), device_id_type=MESH,
                    )
                    copy.start()
                    self.sent.append(copy)
                else:
                    copy = pltpu.make_async_copy(
                        self.stage.at[owner], self.out.at[i, t], self.local.at[i]
                    )
                    copy.start()
                    self.kept.append(copy)

    def finish(self):
        t, nt = self.t, self.nt
        for j in range(1, nt):
            for i in range(self.g):
                slot = self.out.at[i, lax.rem(t - j + nt, nt)]
                pltpu.make_async_copy(slot, slot, self.recv.at[j, i]).wait()
        for copy in self.sent:
            copy.wait_send()
        for copy in self.kept:
            copy.wait()


class Share:
    def __init__(self, nf, src, out, send, recv, pass_send, pass_recv, local):
        self.nf, self.src, self.out = nf, src, out
        self.send, self.recv, self.pass_send, self.pass_recv, self.local = send, recv, pass_send, pass_recv, local
        self.f, self.t = lax.axis_index("fsdp"), lax.axis_index("tensor")
        self.half = nf // 2
        self.chip, self.core = self.f // 2, lax.rem(self.f, 2)
        self.sent = []

    def start(self):
        f, t, half = self.f, self.t, self.half
        for k in range(1, half):
            to = lax.rem(self.chip + k, half) * 2 + self.core
            copy = pltpu.make_async_remote_copy(
                src_ref=self.src, dst_ref=self.out.at[f], send_sem=self.send.at[k], recv_sem=self.recv.at[k],
                device_id=(to, t), device_id_type=MESH,
            )
            copy.start()
            self.sent.append(copy)
        mate = self.chip * 2 + 1 - self.core
        copy = pltpu.make_async_remote_copy(
            src_ref=self.src, dst_ref=self.out.at[f], send_sem=self.pass_send.at[0], recv_sem=self.pass_recv.at[0],
            device_id=(mate, t), device_id_type=MESH,
        )
        copy.start()
        self.sent.append(copy)
        self.own = pltpu.make_async_copy(self.src, self.out.at[f], self.local.at[0])
        self.own.start()

    def forward(self):
        t, half = self.t, self.half
        mate = self.chip * 2 + 1 - self.core
        for k in range(1, half):
            slot = self.out.at[lax.rem(self.chip - k + half, half) * 2 + self.core]
            pltpu.make_async_copy(slot, slot, self.recv.at[k]).wait()
            copy = pltpu.make_async_remote_copy(
                src_ref=slot, dst_ref=slot, send_sem=self.pass_send.at[k], recv_sem=self.pass_recv.at[k],
                device_id=(mate, t), device_id_type=MESH,
            )
            copy.start()
            self.sent.append(copy)

    def finish(self):
        half = self.half
        for k in range(half):
            slot = self.out.at[lax.rem(self.chip - k + half, half) * 2 + 1 - self.core]
            pltpu.make_async_copy(slot, slot, self.pass_recv.at[k]).wait()
        for copy in self.sent:
            copy.wait_send()
        self.own.wait()


def columns_of(ref, width):
    return lambda to: ref.at[:, pl.ds(pl.multiple_of(to * width, width), width)]


def first_kernel(nf, nt, width, w, m, v, hid, cot, w_stage, m_stage, v_stage, w_out, m_out, hid_out, cot_out,
                 send, recv, z_send, z_recv, local, sh_send, sh_recv, ps_send, ps_recv, sh_local):
    greet(nf, nt)
    spread_w = Spread(nf, nt, columns_of(w, width), w_stage, send.at[0], recv.at[0])
    spread_m = Spread(nf, nt, columns_of(m, width), m_stage, send.at[1], recv.at[1])
    spread_v = Spread(nf, nt, columns_of(v, width), v_stage, send.at[2], recv.at[2])
    spread_c = Spread(nf, nt, columns_of(cot, width), cot_out, send.at[3], recv.at[3])
    along_w = Along(nf, nt, w_stage, w_out, z_send.at[0], z_recv.at[0], local.at[0])
    along_m = Along(nf, nt, m_stage, m_out, z_send.at[1], z_recv.at[1], local.at[1])
    share = Share(nf, hid, hid_out, sh_send, sh_recv, ps_send, ps_recv, sh_local)
    spread_w.start()
    spread_m.start()
    along_w.start(spread_w.wait_for)
    share.start()
    spread_c.start()
    along_m.start(spread_m.wait_for)
    spread_v.start()
    share.forward()
    for owner in range(nf):
        spread_c.wait_for(owner)
    for owner in range(nf):
        spread_v.wait_for(owner)
    share.finish()
    along_w.finish()
    along_m.finish()
    for spread in (spread_w, spread_m, spread_v, spread_c):
        spread.finish()


def second_kernel(nf, nt, v_stage, op, hg, op_stage, v_out, op_out, hg_out, send, recv, z_send, z_recv, local):
    greet(nf, nt)
    spread_o = Spread(nf, nt, lambda to: op.at[to], op_stage, send.at[0], recv.at[0])
    spread_h = Spread(nf, nt, lambda to: hg.at[to], hg_out, send.at[1], recv.at[1])
    along_v = Along(nf, nt, v_stage, v_out, z_send.at[0], z_recv.at[0], local.at[0])
    along_o = Along(nf, nt, op_stage, op_out, z_send.at[1], z_recv.at[1], local.at[1])
    spread_o.start()
    along_v.start(None)
    along_o.start(spread_o.wait_for)
    spread_h.start()
    for owner in range(nf):
        spread_h.wait_for(owner)
    along_v.finish()
    along_o.finish()
    spread_o.finish()
    spread_h.finish()


def body(saved_weight, saved_first, saved_second, saved_order, mask, hidden, cotangent):
    nf, nt = lax.axis_size("fsdp"), lax.axis_size("tensor")
    g = nf // nt
    band = saved_order.shape[0]
    width = saved_weight.shape[1] // nf
    tokens, rows = hidden.shape
    scale = (rows * nt) ** (-0.5)
    f32, bf16 = jnp.float32, jnp.bfloat16

    place = (saved_order[None, :] == jnp.arange(band, dtype=saved_order.dtype)[:, None]).astype(bf16)

    def arrange(saved):
        return jnp.dot(place, saved.astype(bf16), preferred_element_type=f32).astype(bf16)

    w, m, v = arrange(saved_weight), arrange(saved_first), arrange(saved_second)

    def shape(*dims):
        return jax.ShapeDtypeStruct(dims, bf16)

    dma = pltpu.SemaphoreType.DMA
    stage, landed = shape(nf, band, width), shape(g, nt, band, width)
    moved = pl.pallas_call(
        functools.partial(first_kernel, nf, nt, width),
        out_shape=(stage, stage, stage, landed, landed, shape(nf, tokens, rows), shape(nf, tokens, width)),
        in_specs=[ANY] * 5,
        out_specs=(ANY,) * 7,
        scratch_shapes=[
            dma((4, nf)), dma((4, nf)), dma((2, nt, g)), dma((2, nt, g)), dma((2, g)),
            dma((nf // 2,)), dma((nf // 2,)), dma((nf // 2,)), dma((nf // 2,)), dma((1,)),
        ],
        compiler_params=pltpu.CompilerParams(collective_id=0, has_side_effects=True),
        name="relay_weight",
    )(w, m, v, hidden, cotangent)
    v_stage, w_out, m_out, hid_all, cot_all = moved[2:]

    weight = w_out.reshape(rows, width)
    masked = jnp.where(mask != 0, weight, jnp.zeros_like(weight))
    part_out = (scale * jnp.dot(hid_all.reshape(nf * tokens, rows), masked, preferred_element_type=f32)).astype(bf16)
    part_grad = (
        scale
        * lax.dot_general(
            cot_all.reshape(nf * tokens, width), masked, (((1,), (1,)), ((), ())), preferred_element_type=f32
        )
    ).astype(bf16)

    moved = pl.pallas_call(
        functools.partial(second_kernel, nf, nt),
        out_shape=(shape(nf, tokens, width), landed, shape(g, nt, tokens, width), shape(nf, tokens, rows)),
        in_specs=[ANY] * 3,
        out_specs=(ANY,) * 4,
        scratch_shapes=[
            dma((2, nf)), dma((2, nf)), dma((2, nt, g)), dma((2, nt, g)), dma((2, g)),
        ],
        compiler_params=pltpu.CompilerParams(collective_id=1, has_side_effects=True),
        name="relay_products",
    )(v_stage, part_out.reshape(nf, tokens, width), part_grad.reshape(nf, tokens, rows))
    v_out, out_parts, grad_parts = moved[1:]

    output = jnp.sum(out_parts.astype(f32), axis=1).astype(bf16)
    output = output.transpose(1, 0, 2).reshape(tokens, g * width)
    hidden_grad = jnp.sum(grad_parts.astype(f32), axis=0).astype(bf16)

    partials = jnp.einsum("ntr,ntc->nrc", hid_all, cot_all, preferred_element_type=f32)
    summed = jnp.sum((scale * partials).astype(bf16).astype(f32), axis=0)
    keep = mask.astype(f32)
    grad = keep * summed
    first = m_out.reshape(rows, width).astype(f32)
    second = v_out.reshape(rows, width).astype(f32)
    new_first = beta_first * first + (1.0 - beta_first) * grad
    new_second = beta_second * second + (1.0 - beta_second) * grad * grad
    corr_first = 1.0 - beta_first ** (STEP + 1)
    corr_second = 1.0 - beta_second ** (STEP + 1)
    update = new_first / corr_first / (jnp.sqrt(new_second / corr_second) + epsilon)
    new_weight = keep * (weight.astype(f32) - learn_rate * (update + decay_rate * weight.astype(f32)))
    return (output, hidden_grad, new_weight, new_first, new_second)


def solution(mesh):
    return jax.shard_map(
        body,
        mesh=mesh,
        in_specs=(
            P(("fsdp", "tensor"), None),
            P(("fsdp", "tensor"), None),
            P(("fsdp", "tensor"), None),
            P(("fsdp", "tensor")),
            P("tensor", "fsdp"),
            P("fsdp", "tensor"),
            P("fsdp", None),
        ),
        out_specs=(
            P("fsdp", "tensor"),
            P("fsdp", "tensor"),
            P("tensor", "fsdp"),
            P("tensor", "fsdp"),
            P("tensor", "fsdp"),
        ),
        check_vma=False,
    )
```

```python
import functools

import jax
import jax.numpy as jnp
from jax import lax
from jax.experimental import pallas as pl
from jax.experimental.pallas import tpu as pltpu
from jax.sharding import PartitionSpec as P

STEP = 1000


beta_first = 0.9
beta_second = 0.999
learn_rate = 0.01
decay_rate = 0.1
epsilon = 1e-08

MESH = pl.DeviceIdType.MESH
ANY = pl.BlockSpec(memory_space=pl.ANY)


def greet(nf, nt):
    f, t = lax.axis_index("fsdp"), lax.axis_index("tensor")
    barrier = pltpu.get_barrier_semaphore()
    for k in range(1, nf):
        pl.semaphore_signal(barrier, inc=1, device_id=(lax.rem(f + k, nf), t), device_id_type=MESH)
    for j in range(1, nt):
        pl.semaphore_signal(barrier, inc=1, device_id=(f, lax.rem(t + j, nt)), device_id_type=MESH)
    pl.semaphore_wait(barrier, nf - 1 + nt - 1)


class Spread:
    def __init__(self, count, me, device_of, block_of, stage, send, recv):
        self.count, self.me, self.device_of = count, me, device_of
        self.block_of, self.stage, self.send, self.recv = block_of, stage, send, recv
        self.sent = []

    def start(self):
        me, count = self.me, self.count
        for k in list(range(2, count)) + [1]:
            to = lax.rem(me + k, count)
            copy = pltpu.make_async_remote_copy(
                src_ref=self.block_of(to), dst_ref=self.stage.at[me],
                send_sem=self.send.at[k], recv_sem=self.recv.at[k],
                device_id=self.device_of(to), device_id_type=MESH,
            )
            copy.start()
            self.sent.append(copy)
        pltpu.make_async_copy(self.block_of(me), self.stage.at[me], self.recv.at[0]).start()

    def wait_for(self, owner):
        slot = self.stage.at[owner]
        pltpu.make_async_copy(slot, slot, self.recv.at[lax.rem(self.me - owner + self.count, self.count)]).wait()

    def finish(self):
        for copy in self.sent:
            copy.wait_send()


class Along:
    def __init__(self, nf, nt, stage, out, send, recv, local):
        self.nf, self.nt, self.stage, self.out = nf, nt, stage, out
        self.send, self.recv, self.local = send, recv, local
        self.f, self.t = lax.axis_index("fsdp"), lax.axis_index("tensor")
        self.g = nf // nt
        self.sent, self.kept = [], []

    def start(self, ready):
        f, t, nt, g = self.f, self.t, self.nt, self.g
        for j in list(range(1, nt)) + [0]:
            to = lax.rem(t + j, nt)
            for i in range(g):
                owner = to * g + i
                if ready is not None:
                    ready(owner)
                if j:
                    copy = pltpu.make_async_remote_copy(
                        src_ref=self.stage.at[owner], dst_ref=self.out.at[i, t],
                        send_sem=self.send.at[j, i], recv_sem=self.recv.at[j, i],
                        device_id=(f, to), device_id_type=MESH,
                    )
                    copy.start()
                    self.sent.append(copy)
                else:
                    copy = pltpu.make_async_copy(
                        self.stage.at[owner], self.out.at[i, t], self.local.at[i]
                    )
                    copy.start()
                    self.kept.append(copy)

    def arrive(self, after=None):
        t, nt = self.t, self.nt
        for j in range(1, nt):
            for i in range(self.g):
                owner = lax.rem(t - j + nt, nt)
                slot = self.out.at[i, owner]
                pltpu.make_async_copy(slot, slot, self.recv.at[j, i]).wait()
                if after is not None:
                    after(i, j, owner)
        for i in range(self.g):
            self.kept[i].wait()
            if after is not None:
                after(i, 0, t)

    def finish(self):
        for copy in self.sent:
            copy.wait_send()


class Share:
    def __init__(self, nf, src, out, send, recv, pass_send, pass_recv, local):
        self.nf, self.src, self.out = nf, src, out
        self.send, self.recv, self.pass_send, self.pass_recv, self.local = send, recv, pass_send, pass_recv, local
        self.f, self.t = lax.axis_index("fsdp"), lax.axis_index("tensor")
        self.half = nf // 2
        self.chip, self.core = self.f // 2, lax.rem(self.f, 2)
        self.sent = []

    def start(self):
        f, t, half = self.f, self.t, self.half
        for k in range(1, half):
            to = lax.rem(self.chip + k, half) * 2 + self.core
            copy = pltpu.make_async_remote_copy(
                src_ref=self.src, dst_ref=self.out.at[f], send_sem=self.send.at[k], recv_sem=self.recv.at[k],
                device_id=(to, t), device_id_type=MESH,
            )
            copy.start()
            self.sent.append(copy)
        mate = self.chip * 2 + 1 - self.core
        copy = pltpu.make_async_remote_copy(
            src_ref=self.src, dst_ref=self.out.at[f], send_sem=self.pass_send.at[0], recv_sem=self.pass_recv.at[0],
            device_id=(mate, t), device_id_type=MESH,
        )
        copy.start()
        self.sent.append(copy)
        self.own = pltpu.make_async_copy(self.src, self.out.at[f], self.local.at[0])
        self.own.start()

    def forward(self):
        t, half = self.t, self.half
        mate = self.chip * 2 + 1 - self.core
        for k in range(1, half):
            slot = self.out.at[lax.rem(self.chip - k + half, half) * 2 + self.core]
            pltpu.make_async_copy(slot, slot, self.recv.at[k]).wait()
            copy = pltpu.make_async_remote_copy(
                src_ref=slot, dst_ref=slot, send_sem=self.pass_send.at[k], recv_sem=self.pass_recv.at[k],
                device_id=(mate, t), device_id_type=MESH,
            )
            copy.start()
            self.sent.append(copy)

    def finish(self):
        half = self.half
        for k in range(half):
            slot = self.out.at[lax.rem(self.chip - k + half, half) * 2 + 1 - self.core]
            pltpu.make_async_copy(slot, slot, self.pass_recv.at[k]).wait()
        for copy in self.sent:
            copy.wait_send()
        self.own.wait()


def columns_of(ref, width, start, size):
    return lambda to: ref.at[:, pl.ds(pl.multiple_of(to * width + start, 128), size)]


def first_kernel(nf, nt, width, w, m, v, keep, hid, cot,
                 w_stage, m_stage, v_stage, w_out, m_out, v_out, hid_out, cot_out, w_mate, cot_mate, keep_mate,
                 send, recv, z_send, z_recv, local, sh_send, sh_recv, ps_send, ps_recv, sh_local,
                 mw_send, mw_recv, mc_send, mc_recv, mk_send, mk_recv):
    f, t = lax.axis_index("fsdp"), lax.axis_index("tensor")
    core = lax.rem(f, 2)
    mate = (f + 1 - 2 * core, t)
    greet(nf, nt)

    def spread(ref, start, size, stage, n):
        return Spread(
            nf, f, lambda to: (to, t), columns_of(ref, width, start, size), stage, send.at[n], recv.at[n]
        )

    def to_mate(src, dst, send_sem, recv_sem):
        copy = pltpu.make_async_remote_copy(
            src_ref=src, dst_ref=dst, send_sem=send_sem, recv_sem=recv_sem, device_id=mate, device_id_type=MESH
        )
        copy.start()
        return copy

    spread_w = spread(w, 0, width, w_stage, 0)
    spread_m = spread(m, 0, width, m_stage, 1)
    spread_v = spread(v, 0, width // 2, v_stage, 2)
    spread_c = spread(cot, 0, width, cot_out, 3)
    along_w = Along(nf, nt, w_stage, w_out, z_send.at[0], z_recv.at[0], local.at[0])
    along_m = Along(nf, nt, m_stage, m_out, z_send.at[1], z_recv.at[1], local.at[1])
    along_v = Along(nf, nt, v_stage, v_out, z_send.at[2], z_recv.at[2], local.at[2])
    share = Share(nf, hid, hid_out, sh_send, sh_recv, ps_send, ps_recv, sh_local)
    passed = []
    spread_w.start()
    spread_m.start()
    passed.append(to_mate(keep, keep_mate, mk_send.at[0], mk_recv.at[0]))
    along_w.start(spread_w.wait_for)
    share.start()
    spread_c.start()
    along_m.start(spread_m.wait_for)
    spread_v.start()
    share.forward()
    along_v.start(spread_v.wait_for)

    def pass_weight(i, j, owner):
        passed.append(to_mate(w_out.at[i, owner], w_mate.at[i, owner], mw_send.at[j, i], mw_recv.at[j, i]))

    along_w.arrive(pass_weight)
    for owner in range(nf):
        spread_c.wait_for(owner)
    for n in range(nf // 2):
        theirs = 2 * n + 1 - core
        passed.append(to_mate(cot_out.at[theirs], cot_mate.at[n], mc_send.at[n], mc_recv.at[n]))
    share.finish()
    for copy in passed:
        copy.wait()
    along_m.arrive()
    along_v.arrive()
    for part in (spread_w, spread_m, spread_v, spread_c, along_w, along_m, along_v):
        part.finish()


def second_kernel(nf, nt, width, v, op, hg, v_stage, op_stage, v_out, op_out, hg_out,
                  send, recv, z_send, z_recv, local):
    f, t = lax.axis_index("fsdp"), lax.axis_index("tensor")
    chip, core = f // 2, lax.rem(f, 2)
    greet(nf, nt)
    everyone = lambda to: (to, t)
    spread_v = Spread(
        nf, f, everyone, columns_of(v, width, width // 2, width // 2), v_stage, send.at[0], recv.at[0]
    )
    spread_o = Spread(nf, f, everyone, lambda to: op.at[to], op_stage, send.at[1], recv.at[1])
    spread_h = Spread(
        nf // 2, chip, lambda to: (to * 2 + core, t), lambda to: hg.at[to], hg_out, send.at[2], recv.at[2]
    )
    along_v = Along(nf, nt, v_stage, v_out, z_send.at[0], z_recv.at[0], local.at[0])
    along_o = Along(nf, nt, op_stage, op_out, z_send.at[1], z_recv.at[1], local.at[1])
    spread_v.start()
    spread_o.start()
    along_v.start(spread_v.wait_for)
    along_o.start(spread_o.wait_for)
    spread_h.start()
    for owner in range(nf // 2):
        spread_h.wait_for(owner)
    along_v.arrive()
    along_o.arrive()
    for part in (spread_v, spread_o, spread_h, along_v, along_o):
        part.finish()


def step_kernel(scale, hid, cot, mask, w, m, va, vb, new_w, new_m, new_v):
    f32 = jnp.float32
    blocks, _, width = cot.shape
    piece = width // 4
    corr_first = 1.0 - beta_first ** (STEP + 1)
    corr_second = 1.0 - beta_second ** (STEP + 1)
    for c in range(4):
        cols = slice(c * piece, (c + 1) * piece)
        total = None
        for n in range(blocks):
            part = lax.dot_general(
                hid[n], cot[n, :, cols], (((0,), (0,)), ((), ())), preferred_element_type=f32
            )
            part = (scale * part).astype(jnp.bfloat16).astype(f32)
            total = part if total is None else total + part
        kept = mask[:, cols] != 0
        grad = jnp.where(kept, total, 0.0)
        half = slice((c % 2) * piece, (c % 2 + 1) * piece)
        second = (va if c < 2 else vb)[:, half].astype(f32)
        weight = w[:, cols].astype(f32)
        first = beta_first * m[:, cols].astype(f32) + (1.0 - beta_first) * grad
        second = beta_second * second + (1.0 - beta_second) * grad * grad
        update = (first * (1.0 / corr_first)) / (jnp.sqrt(second * (1.0 / corr_second)) + epsilon)
        new_m[:, cols] = first
        new_v[:, cols] = second
        new_w[:, cols] = jnp.where(kept, weight - learn_rate * (update + decay_rate * weight), 0.0)


def body(saved_weight, saved_first, saved_second, saved_order, mask, hidden, cotangent):
    nf, nt = lax.axis_size("fsdp"), lax.axis_size("tensor")
    g = nf // nt
    band = saved_order.shape[0]
    width = saved_weight.shape[1] // nf
    tokens, rows = hidden.shape
    scale = (rows * nt) ** (-0.5)
    f32, bf16 = jnp.float32, jnp.bfloat16

    place = (saved_order[None, :] == jnp.arange(band, dtype=saved_order.dtype)[:, None]).astype(bf16)

    def arrange(saved):
        return jnp.dot(place, saved.astype(bf16), preferred_element_type=f32).astype(bf16)

    w, m, v = arrange(saved_weight), arrange(saved_first), arrange(saved_second)

    def shape(*dims):
        return jax.ShapeDtypeStruct(dims, bf16)

    dma = pltpu.SemaphoreType.DMA
    half = width // 2
    stage, landed = shape(nf, band, width), shape(g, nt, band, width)
    stage_half, landed_half = shape(nf, band, half), shape(g, nt, band, half)
    keep = mask.astype(bf16)
    moved = pl.pallas_call(
        functools.partial(first_kernel, nf, nt, width),
        out_shape=(
            stage, stage, stage_half, landed, landed, landed_half, shape(nf, tokens, rows), shape(nf, tokens, width),
            landed, shape(nf // 2, tokens, width), shape(rows, width),
        ),
        in_specs=[ANY] * 6,
        out_specs=(ANY,) * 11,
        scratch_shapes=[
            dma((4, nf)), dma((4, nf)), dma((3, nt, g)), dma((3, nt, g)), dma((3, g)),
            dma((nf // 2,)), dma((nf // 2,)), dma((nf // 2,)), dma((nf // 2,)), dma((1,)),
            dma((nt, g)), dma((nt, g)), dma((nf // 2,)), dma((nf // 2,)), dma((1,)), dma((1,)),
        ],
        compiler_params=pltpu.CompilerParams(collective_id=0, has_side_effects=True),
        name="relay_weight",
    )(w, m, v, keep, hidden, cotangent)
    w_out, m_out, va_out, hid_all, cot_all, w_mate, cot_mate, keep_mate = moved[3:]

    weight = w_out.reshape(rows, width)
    masked = weight * keep
    masked_mate = w_mate.reshape(rows, width) * keep_mate
    part_out = (scale * jnp.dot(hid_all.reshape(nf * tokens, rows), masked, preferred_element_type=f32)).astype(bf16)
    core = lax.rem(lax.axis_index("fsdp"), 2)
    cot_own = lax.dynamic_index_in_dim(cot_all.reshape(nf // 2, 2, tokens, width), core, 1, keepdims=False)

    def back(cot, masked):
        return lax.dot_general(
            cot.reshape(nf // 2 * tokens, width), masked, (((1,), (1,)), ((), ())), preferred_element_type=f32
        )

    part_grad = (scale * (back(cot_own, masked) + back(cot_mate, masked_mate))).astype(bf16)

    moved = pl.pallas_call(
        functools.partial(second_kernel, nf, nt, width),
        out_shape=(
            stage_half, shape(nf, tokens, width), landed_half, shape(g, nt, tokens, width),
            shape(nf // 2, tokens, rows),
        ),
        in_specs=[ANY] * 3,
        out_specs=(ANY,) * 5,
        scratch_shapes=[
            dma((3, nf)), dma((3, nf)), dma((2, nt, g)), dma((2, nt, g)), dma((2, g)),
        ],
        compiler_params=pltpu.CompilerParams(collective_id=1, has_side_effects=True),
        name="relay_products",
    )(v, part_out.reshape(nf, tokens, width), part_grad.reshape(nf // 2, tokens, rows))
    vb_out, out_parts, grad_parts = moved[2:]

    output = jnp.sum(out_parts.astype(f32), axis=1).astype(bf16)
    output = output.transpose(1, 0, 2).reshape(tokens, g * width)
    hidden_grad = jnp.sum(grad_parts.astype(f32), axis=0).astype(bf16)

    tile = 256 if rows % 256 == 0 else 128
    whole = lambda cols: pl.BlockSpec((tile, cols), lambda r: (r, 0))
    result = jax.ShapeDtypeStruct((rows, width), f32)
    new_weight, new_first, new_second = pl.pallas_call(
        functools.partial(step_kernel, scale),
        grid=(rows // tile,),
        out_shape=(result,) * 3,
        in_specs=[
            pl.BlockSpec((nf, tokens, tile), lambda r: (0, 0, r)),
            pl.BlockSpec((nf, tokens, width), lambda r: (0, 0, 0)),
            whole(width), whole(width), whole(width), whole(half), whole(half),
        ],
        out_specs=(whole(width),) * 3,
        compiler_params=pltpu.CompilerParams(vmem_limit_bytes=48 * 2**20),
        name="grad_and_step",
    )(
        hid_all, cot_all, mask, weight, m_out.reshape(rows, width),
        va_out.reshape(rows, half), vb_out.reshape(rows, half),
    )
    return (output, hidden_grad, new_weight, new_first, new_second)


def solution(mesh):
    return jax.shard_map(
        body,
        mesh=mesh,
        in_specs=(
            P(("fsdp", "tensor"), None),
            P(("fsdp", "tensor"), None),
            P(("fsdp", "tensor"), None),
            P(("fsdp", "tensor")),
            P("tensor", "fsdp"),
            P("fsdp", "tensor"),
            P("fsdp", None),
        ),
        out_specs=(
            P("fsdp", "tensor"),
            P("fsdp", "tensor"),
            P("tensor", "fsdp"),
            P("tensor", "fsdp"),
            P("tensor", "fsdp"),
        ),
        check_vma=False,
    )
```

```python
import functools

import jax
import jax.numpy as jnp
from jax import lax
from jax.experimental import pallas as pl
from jax.experimental.pallas import tpu as pltpu
from jax.sharding import PartitionSpec as P

STEP = 1000


beta_first = 0.9
beta_second = 0.999
learn_rate = 0.01
decay_rate = 0.1
epsilon = 1e-08

MESH = pl.DeviceIdType.MESH
ANY = pl.BlockSpec(memory_space=pl.ANY)


def greet(nf, nt):
    f, t = lax.axis_index("fsdp"), lax.axis_index("tensor")
    barrier = pltpu.get_barrier_semaphore()
    for k in range(1, nf):
        pl.semaphore_signal(barrier, inc=1, device_id=(lax.rem(f + k, nf), t), device_id_type=MESH)
    for j in range(1, nt):
        pl.semaphore_signal(barrier, inc=1, device_id=(f, lax.rem(t + j, nt)), device_id_type=MESH)
    pl.semaphore_wait(barrier, nf - 1 + nt - 1)


class Spread:
    def __init__(self, count, me, device_of, block_of, stage, send, recv):
        self.count, self.me, self.device_of = count, me, device_of
        self.block_of, self.stage, self.send, self.recv = block_of, stage, send, recv
        self.sent = []

    def start(self):
        me, count = self.me, self.count
        for k in list(range(2, count)) + [1]:
            to = lax.rem(me + k, count)
            copy = pltpu.make_async_remote_copy(
                src_ref=self.block_of(to), dst_ref=self.stage.at[me],
                send_sem=self.send.at[k], recv_sem=self.recv.at[k],
                device_id=self.device_of(to), device_id_type=MESH,
            )
            copy.start()
            self.sent.append(copy)
        pltpu.make_async_copy(self.block_of(me), self.stage.at[me], self.recv.at[0]).start()

    def wait_for(self, owner):
        slot = self.stage.at[owner]
        pltpu.make_async_copy(slot, slot, self.recv.at[lax.rem(self.me - owner + self.count, self.count)]).wait()

    def finish(self):
        for copy in self.sent:
            copy.wait_send()


class Along:
    def __init__(self, nf, nt, stage, out, send, recv, local):
        self.nf, self.nt, self.stage, self.out = nf, nt, stage, out
        self.send, self.recv, self.local = send, recv, local
        self.f, self.t = lax.axis_index("fsdp"), lax.axis_index("tensor")
        self.g = nf // nt
        self.sent, self.kept = [], []

    def start(self, ready):
        f, t, nt, g = self.f, self.t, self.nt, self.g
        for j in list(range(1, nt)) + [0]:
            to = lax.rem(t + j, nt)
            for i in range(g):
                owner = to * g + i
                if ready is not None:
                    ready(owner)
                if j:
                    copy = pltpu.make_async_remote_copy(
                        src_ref=self.stage.at[owner], dst_ref=self.out.at[i, t],
                        send_sem=self.send.at[j, i], recv_sem=self.recv.at[j, i],
                        device_id=(f, to), device_id_type=MESH,
                    )
                    copy.start()
                    self.sent.append(copy)
                else:
                    copy = pltpu.make_async_copy(
                        self.stage.at[owner], self.out.at[i, t], self.local.at[i]
                    )
                    copy.start()
                    self.kept.append(copy)

    def arrive(self, after=None):
        t, nt = self.t, self.nt
        for j in range(1, nt):
            for i in range(self.g):
                owner = lax.rem(t - j + nt, nt)
                slot = self.out.at[i, owner]
                pltpu.make_async_copy(slot, slot, self.recv.at[j, i]).wait()
                if after is not None:
                    after(i, j, owner)
        for i in range(self.g):
            self.kept[i].wait()
            if after is not None:
                after(i, 0, t)

    def finish(self):
        for copy in self.sent:
            copy.wait_send()


class Share:
    def __init__(self, nf, src, out, send, recv, pass_send, pass_recv, local):
        self.nf, self.src, self.out = nf, src, out
        self.send, self.recv, self.pass_send, self.pass_recv, self.local = send, recv, pass_send, pass_recv, local
        self.f, self.t = lax.axis_index("fsdp"), lax.axis_index("tensor")
        self.half = nf // 2
        self.chip, self.core = self.f // 2, lax.rem(self.f, 2)
        self.sent = []

    def start(self):
        f, t, half = self.f, self.t, self.half
        for k in range(1, half):
            to = lax.rem(self.chip + k, half) * 2 + self.core
            copy = pltpu.make_async_remote_copy(
                src_ref=self.src, dst_ref=self.out.at[f], send_sem=self.send.at[k], recv_sem=self.recv.at[k],
                device_id=(to, t), device_id_type=MESH,
            )
            copy.start()
            self.sent.append(copy)
        mate = self.chip * 2 + 1 - self.core
        copy = pltpu.make_async_remote_copy(
            src_ref=self.src, dst_ref=self.out.at[f], send_sem=self.pass_send.at[0], recv_sem=self.pass_recv.at[0],
            device_id=(mate, t), device_id_type=MESH,
        )
        copy.start()
        self.sent.append(copy)
        self.own = pltpu.make_async_copy(self.src, self.out.at[f], self.local.at[0])
        self.own.start()

    def forward(self):
        t, half = self.t, self.half
        mate = self.chip * 2 + 1 - self.core
        for k in range(1, half):
            slot = self.out.at[lax.rem(self.chip - k + half, half) * 2 + self.core]
            pltpu.make_async_copy(slot, slot, self.recv.at[k]).wait()
            copy = pltpu.make_async_remote_copy(
                src_ref=slot, dst_ref=slot, send_sem=self.pass_send.at[k], recv_sem=self.pass_recv.at[k],
                device_id=(mate, t), device_id_type=MESH,
            )
            copy.start()
            self.sent.append(copy)

    def finish(self):
        half = self.half
        for k in range(half):
            slot = self.out.at[lax.rem(self.chip - k + half, half) * 2 + 1 - self.core]
            pltpu.make_async_copy(slot, slot, self.pass_recv.at[k]).wait()
        for copy in self.sent:
            copy.wait_send()
        self.own.wait()


def columns_of(ref, width, start, size):
    return lambda to: ref.at[:, pl.ds(pl.multiple_of(to * width + start, 128), size)]


def first_kernel(nf, nt, width, w, m, v, keep, hid, cot,
                 w_stage, m_stage, v_stage, w_out, m_out, v_out, hid_out, cot_out, w_mate, cot_mate, keep_mate, v_later,
                 send, recv, z_send, z_recv, local, sh_send, sh_recv, ps_send, ps_recv, sh_local,
                 mw_send, mw_recv, mc_send, mc_recv, mk_send, mk_recv):
    f, t = lax.axis_index("fsdp"), lax.axis_index("tensor")
    core = lax.rem(f, 2)
    mate = (f + 1 - 2 * core, t)
    greet(nf, nt)

    def spread(ref, start, size, stage, n):
        return Spread(
            nf, f, lambda to: (to, t), columns_of(ref, width, start, size), stage, send.at[n], recv.at[n]
        )

    def to_mate(src, dst, send_sem, recv_sem):
        copy = pltpu.make_async_remote_copy(
            src_ref=src, dst_ref=dst, send_sem=send_sem, recv_sem=recv_sem, device_id=mate, device_id_type=MESH
        )
        copy.start()
        return copy

    spread_w = spread(w, 0, width, w_stage, 0)
    spread_m = spread(m, 0, width, m_stage, 1)
    spread_v = spread(v, 0, width // 2, v_stage, 2)
    spread_c = spread(cot, 0, width, cot_out, 3)
    spread_l = spread(v, width // 2, width // 4, v_later, 4)
    along_w = Along(nf, nt, w_stage, w_out, z_send.at[0], z_recv.at[0], local.at[0])
    along_m = Along(nf, nt, m_stage, m_out, z_send.at[1], z_recv.at[1], local.at[1])
    along_v = Along(nf, nt, v_stage, v_out, z_send.at[2], z_recv.at[2], local.at[2])
    share = Share(nf, hid, hid_out, sh_send, sh_recv, ps_send, ps_recv, sh_local)
    passed = []
    spread_w.start()
    spread_m.start()
    passed.append(to_mate(keep, keep_mate, mk_send.at[0], mk_recv.at[0]))
    along_w.start(spread_w.wait_for)
    share.start()
    spread_c.start()
    along_m.start(spread_m.wait_for)
    spread_v.start()
    share.forward()
    along_v.start(spread_v.wait_for)
    spread_l.start()

    def pass_weight(i, j, owner):
        passed.append(to_mate(w_out.at[i, owner], w_mate.at[i, owner], mw_send.at[j, i], mw_recv.at[j, i]))

    along_w.arrive(pass_weight)
    for owner in range(nf):
        spread_c.wait_for(owner)
    for n in range(nf // 2):
        theirs = 2 * n + 1 - core
        passed.append(to_mate(cot_out.at[theirs], cot_mate.at[n], mc_send.at[n], mc_recv.at[n]))
    share.finish()
    for copy in passed:
        copy.wait()
    along_m.arrive()
    along_v.arrive()
    for owner in range(nf):
        spread_l.wait_for(owner)
    for part in (spread_w, spread_m, spread_v, spread_c, spread_l, along_w, along_m, along_v):
        part.finish()


def second_kernel(nf, nt, width, v, op, hg, v_stage, op_stage, v_out, op_out, hg_out, op_later,
                  send, recv, z_send, z_recv, local):
    f, t = lax.axis_index("fsdp"), lax.axis_index("tensor")
    chip, core = f // 2, lax.rem(f, 2)
    greet(nf, nt)
    everyone = lambda to: (to, t)
    spread_v = Spread(
        nf, f, everyone, columns_of(v, width, width // 2 + width // 4, width // 4), v_stage, send.at[0], recv.at[0]
    )
    now, later = op_stage.shape[1], op_later.shape[1]
    spread_o = Spread(nf, f, everyone, lambda to: op.at[to, pl.ds(0, now)], op_stage, send.at[1], recv.at[1])
    spread_l = Spread(nf, f, everyone, lambda to: op.at[to, pl.ds(now, later)], op_later, send.at[3], recv.at[3])
    spread_h = Spread(
        nf // 2, chip, lambda to: (to * 2 + core, t), lambda to: hg.at[to], hg_out, send.at[2], recv.at[2]
    )
    along_v = Along(nf, nt, v_stage, v_out, z_send.at[0], z_recv.at[0], local.at[0])
    along_o = Along(nf, nt, op_stage, op_out, z_send.at[1], z_recv.at[1], local.at[1])
    spread_v.start()
    spread_o.start()
    along_v.start(spread_v.wait_for)
    along_o.start(spread_o.wait_for)
    spread_l.start()
    spread_h.start()
    for owner in range(nf):
        spread_l.wait_for(owner)
    for owner in range(nf // 2):
        spread_h.wait_for(owner)
    along_v.arrive()
    along_o.arrive()
    for part in (spread_v, spread_o, spread_l, spread_h, along_v, along_o):
        part.finish()


def step_kernel(scale, hid, cot, mask, w, m, va, vl, vb, new_w, new_m, new_v):
    f32 = jnp.float32
    blocks, _, width = cot.shape
    piece = width // 4
    corr_first = 1.0 - beta_first ** (STEP + 1)
    corr_second = 1.0 - beta_second ** (STEP + 1)
    for c in range(4):
        cols = slice(c * piece, (c + 1) * piece)
        total = None
        for n in range(blocks):
            part = lax.dot_general(
                hid[n], cot[n, :, cols], (((0,), (0,)), ((), ())), preferred_element_type=f32
            )
            part = (scale * part).astype(jnp.bfloat16).astype(f32)
            total = part if total is None else total + part
        kept = mask[:, cols] != 0
        grad = jnp.where(kept, total, 0.0)
        second = (va[:, cols] if c < 2 else vl[...] if c == 2 else vb[...]).astype(f32)
        weight = w[:, cols].astype(f32)
        first = beta_first * m[:, cols].astype(f32) + (1.0 - beta_first) * grad
        second = beta_second * second + (1.0 - beta_second) * grad * grad
        update = (first * (1.0 / corr_first)) / (jnp.sqrt(second * (1.0 / corr_second)) + epsilon)
        new_m[:, cols] = first
        new_v[:, cols] = second
        new_w[:, cols] = jnp.where(kept, weight - learn_rate * (update + decay_rate * weight), 0.0)


def body(saved_weight, saved_first, saved_second, saved_order, mask, hidden, cotangent):
    nf, nt = lax.axis_size("fsdp"), lax.axis_size("tensor")
    g = nf // nt
    band = saved_order.shape[0]
    width = saved_weight.shape[1] // nf
    tokens, rows = hidden.shape
    scale = (rows * nt) ** (-0.5)
    f32, bf16 = jnp.float32, jnp.bfloat16

    place = (saved_order[None, :] == jnp.arange(band, dtype=saved_order.dtype)[:, None]).astype(bf16)

    def arrange(saved):
        return jnp.dot(place, saved.astype(bf16), preferred_element_type=f32).astype(bf16)

    w, m, v = arrange(saved_weight), arrange(saved_first), arrange(saved_second)

    def shape(*dims):
        return jax.ShapeDtypeStruct(dims, bf16)

    def hop(stage):
        slots = stage.reshape((nt, g) + stage.shape[1:])
        pick = lambda j: lax.dynamic_index_in_dim(slots, lax.rem(t + j, nt), 0, keepdims=False)
        return [pick(0)] + [
            lax.ppermute(pick(j), "tensor", [(n, (n + j) % nt) for n in range(nt)]) for j in range(1, nt)
        ]

    def arranged(pieces):
        stacked = jnp.stack(pieces)
        return [
            lax.dynamic_index_in_dim(stacked, lax.rem(t - n + nt, nt), 0, keepdims=False) for n in range(nt)
        ]

    dma = pltpu.SemaphoreType.DMA
    t = lax.axis_index("tensor")
    half = width // 2
    stage, landed = shape(nf, band, width), shape(g, nt, band, width)
    stage_half, landed_half = shape(nf, band, half), shape(g, nt, band, half)
    keep = mask.astype(bf16)
    moved = pl.pallas_call(
        functools.partial(first_kernel, nf, nt, width),
        out_shape=(
            stage, stage, stage_half, landed, landed, landed_half, shape(nf, tokens, rows), shape(nf, tokens, width),
            landed, shape(nf // 2, tokens, width), shape(rows, width),
            shape(nf, band, width // 4),
        ),
        in_specs=[ANY] * 6,
        out_specs=(ANY,) * 12,
        scratch_shapes=[
            dma((5, nf)), dma((5, nf)), dma((3, nt, g)), dma((3, nt, g)), dma((3, g)),
            dma((nf // 2,)), dma((nf // 2,)), dma((nf // 2,)), dma((nf // 2,)), dma((1,)),
            dma((nt, g)), dma((nt, g)), dma((nf // 2,)), dma((nf // 2,)), dma((1,)), dma((1,)),
        ],
        compiler_params=pltpu.CompilerParams(collective_id=0, has_side_effects=True),
        name="relay_weight",
    )(w, m, v, keep, hidden, cotangent)
    w_out, m_out, va_out, hid_all, cot_all, w_mate, cot_mate, keep_mate, v_later = moved[3:]
    vl_out = jnp.stack(arranged(hop(v_later)), axis=1)

    weight = w_out.reshape(rows, width)
    masked = weight * keep
    masked_mate = w_mate.reshape(rows, width) * keep_mate
    part_out = (scale * jnp.dot(hid_all.reshape(nf * tokens, rows), masked, preferred_element_type=f32)).astype(bf16)
    core = lax.rem(lax.axis_index("fsdp"), 2)
    cot_own = lax.dynamic_index_in_dim(cot_all.reshape(nf // 2, 2, tokens, width), core, 1, keepdims=False)

    def back(cot, masked):
        return lax.dot_general(
            cot.reshape(nf // 2 * tokens, width), masked, (((1,), (1,)), ((), ())), preferred_element_type=f32
        )

    part_grad = (scale * (back(cot_own, masked) + back(cot_mate, masked_mate))).astype(bf16)

    later = tokens * 3 // 8 // 16 * 16
    now = tokens - later
    moved = pl.pallas_call(
        functools.partial(second_kernel, nf, nt, width),
        out_shape=(
            shape(nf, band, width // 4), shape(nf, now, width), shape(g, nt, band, width // 4),
            shape(g, nt, now, width), shape(nf // 2, tokens, rows), shape(nf, later, width),
        ),
        in_specs=[ANY] * 3,
        out_specs=(ANY,) * 6,
        scratch_shapes=[
            dma((4, nf)), dma((4, nf)), dma((2, nt, g)), dma((2, nt, g)), dma((2, g)),
        ],
        compiler_params=pltpu.CompilerParams(collective_id=1, has_side_effects=True),
        name="relay_products",
    )(v, part_out.reshape(nf, tokens, width), part_grad.reshape(nf // 2, tokens, rows))
    vb_out, out_parts, grad_parts, out_later = moved[2:]
    out_later = hop(out_later)

    hidden_grad = jnp.sum(grad_parts.astype(f32), axis=0).astype(bf16)

    tile = 256 if rows % 256 == 0 else 128
    whole = lambda cols: pl.BlockSpec((tile, cols), lambda r: (r, 0))
    result = jax.ShapeDtypeStruct((rows, width), f32)
    new_weight, new_first, new_second = pl.pallas_call(
        functools.partial(step_kernel, scale),
        grid=(rows // tile,),
        out_shape=(result,) * 3,
        in_specs=[
            pl.BlockSpec((nf, tokens, tile), lambda r: (0, 0, r)),
            pl.BlockSpec((nf, tokens, width), lambda r: (0, 0, 0)),
            whole(width), whole(width), whole(width), whole(half), whole(width // 4), whole(width // 4),
        ],
        out_specs=(whole(width),) * 3,
        compiler_params=pltpu.CompilerParams(vmem_limit_bytes=48 * 2**20),
        cost_estimate=pl.CostEstimate(
            flops=2 * nf * tokens * rows * width, bytes_accessed=50 * rows * width // 2, transcendentals=rows * width
        ),
        name="grad_and_step",
    )(
        hid_all, cot_all, mask, weight, m_out.reshape(rows, width),
        va_out.reshape(rows, half), vl_out.reshape(rows, width // 4), vb_out.reshape(rows, width // 4),
    )
    output = jnp.concatenate(
        [jnp.sum(out_parts.astype(f32), axis=1), sum(piece.astype(f32) for piece in out_later)], axis=1
    ).astype(bf16)
    output = output.transpose(1, 0, 2).reshape(tokens, g * width)
    return (output, hidden_grad, new_weight, new_first, new_second)


def solution(mesh):
    return jax.shard_map(
        body,
        mesh=mesh,
        in_specs=(
            P(("fsdp", "tensor"), None),
            P(("fsdp", "tensor"), None),
            P(("fsdp", "tensor"), None),
            P(("fsdp", "tensor")),
            P("tensor", "fsdp"),
            P("fsdp", "tensor"),
            P("fsdp", None),
        ),
        out_specs=(
            P("fsdp", "tensor"),
            P("fsdp", "tensor"),
            P("tensor", "fsdp"),
            P("tensor", "fsdp"),
            P("tensor", "fsdp"),
        ),
        check_vma=False,
    )
```

```python
import functools

import jax
import jax.numpy as jnp
from jax import lax
from jax.experimental import pallas as pl
from jax.experimental.pallas import tpu as pltpu
from jax.sharding import PartitionSpec as P

STEP = 1000


beta_first = 0.9
beta_second = 0.999
learn_rate = 0.01
decay_rate = 0.1
epsilon = 1e-08

MESH = pl.DeviceIdType.MESH
ANY = pl.BlockSpec(memory_space=pl.ANY)


def greet(nf, nt):
    f, t = lax.axis_index("fsdp"), lax.axis_index("tensor")
    barrier = pltpu.get_barrier_semaphore()
    for k in range(1, nf):
        pl.semaphore_signal(barrier, inc=1, device_id=(lax.rem(f + k, nf), t), device_id_type=MESH)
    for j in range(1, nt):
        pl.semaphore_signal(barrier, inc=1, device_id=(f, lax.rem(t + j, nt)), device_id_type=MESH)
    pl.semaphore_wait(barrier, nf - 1 + nt - 1)


class Spread:
    def __init__(self, count, me, device_of, block_of, stage, send, recv):
        self.count, self.me, self.device_of = count, me, device_of
        self.block_of, self.stage, self.send, self.recv = block_of, stage, send, recv
        self.sent = []

    def start(self):
        me, count = self.me, self.count
        for k in list(range(2, count)) + [1]:
            to = lax.rem(me + k, count)
            copy = pltpu.make_async_remote_copy(
                src_ref=self.block_of(to), dst_ref=self.stage.at[me],
                send_sem=self.send.at[k], recv_sem=self.recv.at[k],
                device_id=self.device_of(to), device_id_type=MESH,
            )
            copy.start()
            self.sent.append(copy)
        pltpu.make_async_copy(self.block_of(me), self.stage.at[me], self.recv.at[0]).start()

    def wait_for(self, owner):
        slot = self.stage.at[owner]
        pltpu.make_async_copy(slot, slot, self.recv.at[lax.rem(self.me - owner + self.count, self.count)]).wait()

    def finish(self):
        for copy in self.sent:
            copy.wait_send()


class Along:
    def __init__(self, nf, nt, stage, out, send, recv, local):
        self.nf, self.nt, self.stage, self.out = nf, nt, stage, out
        self.send, self.recv, self.local = send, recv, local
        self.f, self.t = lax.axis_index("fsdp"), lax.axis_index("tensor")
        self.g = nf // nt
        self.sent, self.kept = [], []

    def start(self, ready):
        f, t, nt, g = self.f, self.t, self.nt, self.g
        for j in list(range(1, nt)) + [0]:
            to = lax.rem(t + j, nt)
            for i in range(g):
                owner = to * g + i
                if ready is not None:
                    ready(owner)
                if j:
                    copy = pltpu.make_async_remote_copy(
                        src_ref=self.stage.at[owner], dst_ref=self.out.at[i, t],
                        send_sem=self.send.at[j, i], recv_sem=self.recv.at[j, i],
                        device_id=(f, to), device_id_type=MESH,
                    )
                    copy.start()
                    self.sent.append(copy)
                else:
                    copy = pltpu.make_async_copy(
                        self.stage.at[owner], self.out.at[i, t], self.local.at[i]
                    )
                    copy.start()
                    self.kept.append(copy)

    def arrive(self, after=None):
        t, nt = self.t, self.nt
        for j in range(1, nt):
            for i in range(self.g):
                owner = lax.rem(t - j + nt, nt)
                slot = self.out.at[i, owner]
                pltpu.make_async_copy(slot, slot, self.recv.at[j, i]).wait()
                if after is not None:
                    after(i, j, owner)
        for i in range(self.g):
            self.kept[i].wait()
            if after is not None:
                after(i, 0, t)

    def finish(self):
        for copy in self.sent:
            copy.wait_send()


class Share:
    def __init__(self, nf, src, out, send, recv, pass_send, pass_recv, local):
        self.nf, self.src, self.out = nf, src, out
        self.send, self.recv, self.pass_send, self.pass_recv, self.local = send, recv, pass_send, pass_recv, local
        self.f, self.t = lax.axis_index("fsdp"), lax.axis_index("tensor")
        self.half = nf // 2
        self.chip, self.core = self.f // 2, lax.rem(self.f, 2)
        self.sent = []

    def start(self):
        f, t, half = self.f, self.t, self.half
        for k in range(1, half):
            to = lax.rem(self.chip + k, half) * 2 + self.core
            copy = pltpu.make_async_remote_copy(
                src_ref=self.src, dst_ref=self.out.at[f], send_sem=self.send.at[k], recv_sem=self.recv.at[k],
                device_id=(to, t), device_id_type=MESH,
            )
            copy.start()
            self.sent.append(copy)
        mate = self.chip * 2 + 1 - self.core
        copy = pltpu.make_async_remote_copy(
            src_ref=self.src, dst_ref=self.out.at[f], send_sem=self.pass_send.at[0], recv_sem=self.pass_recv.at[0],
            device_id=(mate, t), device_id_type=MESH,
        )
        copy.start()
        self.sent.append(copy)
        self.own = pltpu.make_async_copy(self.src, self.out.at[f], self.local.at[0])
        self.own.start()

    def forward(self):
        t, half = self.t, self.half
        mate = self.chip * 2 + 1 - self.core
        for k in range(1, half):
            slot = self.out.at[lax.rem(self.chip - k + half, half) * 2 + self.core]
            pltpu.make_async_copy(slot, slot, self.recv.at[k]).wait()
            copy = pltpu.make_async_remote_copy(
                src_ref=slot, dst_ref=slot, send_sem=self.pass_send.at[k], recv_sem=self.pass_recv.at[k],
                device_id=(mate, t), device_id_type=MESH,
            )
            copy.start()
            self.sent.append(copy)

    def finish(self):
        half = self.half
        for k in range(half):
            slot = self.out.at[lax.rem(self.chip - k + half, half) * 2 + 1 - self.core]
            pltpu.make_async_copy(slot, slot, self.pass_recv.at[k]).wait()
        for copy in self.sent:
            copy.wait_send()
        self.own.wait()


def columns_of(ref, width, start, size):
    return lambda to: ref.at[:, pl.ds(pl.multiple_of(to * width + start, 128), size)]


def first_kernel(nf, nt, width, w, m, v, keep, hid, cot,
                 w_stage, m_stage, v_stage, w_out, m_out, v_out, hid_out, cot_out, w_mate, cot_mate, keep_mate, v_later,
                 send, recv, z_send, z_recv, local, sh_send, sh_recv, ps_send, ps_recv, sh_local,
                 mw_send, mw_recv, mc_send, mc_recv, mk_send, mk_recv):
    f, t = lax.axis_index("fsdp"), lax.axis_index("tensor")
    core = lax.rem(f, 2)
    mate = (f + 1 - 2 * core, t)
    greet(nf, nt)

    def spread(ref, start, size, stage, n):
        return Spread(
            nf, f, lambda to: (to, t), columns_of(ref, width, start, size), stage, send.at[n], recv.at[n]
        )

    def to_mate(src, dst, send_sem, recv_sem):
        copy = pltpu.make_async_remote_copy(
            src_ref=src, dst_ref=dst, send_sem=send_sem, recv_sem=recv_sem, device_id=mate, device_id_type=MESH
        )
        copy.start()
        return copy

    spread_w = spread(w, 0, width, w_stage, 0)
    spread_m = spread(m, 0, width, m_stage, 1)
    spread_v = spread(v, 0, width // 4, v_stage, 2)
    spread_c = spread(cot, 0, width, cot_out, 3)
    spread_l = spread(v, width // 4, width // 2, v_later, 4)
    along_w = Along(nf, nt, w_stage, w_out, z_send.at[0], z_recv.at[0], local.at[0])
    along_m = Along(nf, nt, m_stage, m_out, z_send.at[1], z_recv.at[1], local.at[1])
    along_v = Along(nf, nt, v_stage, v_out, z_send.at[2], z_recv.at[2], local.at[2])
    share = Share(nf, hid, hid_out, sh_send, sh_recv, ps_send, ps_recv, sh_local)
    passed = []
    spread_w.start()
    spread_m.start()
    passed.append(to_mate(keep, keep_mate, mk_send.at[0], mk_recv.at[0]))
    along_w.start(spread_w.wait_for)
    share.start()
    spread_c.start()
    along_m.start(spread_m.wait_for)
    spread_v.start()
    share.forward()
    along_v.start(spread_v.wait_for)
    spread_l.start()

    def pass_weight(i, j, owner):
        passed.append(to_mate(w_out.at[i, owner], w_mate.at[i, owner], mw_send.at[j, i], mw_recv.at[j, i]))

    along_w.arrive(pass_weight)
    for owner in range(nf):
        spread_c.wait_for(owner)
    for n in range(nf // 2):
        theirs = 2 * n + 1 - core
        passed.append(to_mate(cot_out.at[theirs], cot_mate.at[n], mc_send.at[n], mc_recv.at[n]))
    share.finish()
    for copy in passed:
        copy.wait()
    along_m.arrive()
    along_v.arrive()
    for owner in range(nf):
        spread_l.wait_for(owner)
    for part in (spread_w, spread_m, spread_v, spread_c, spread_l, along_w, along_m, along_v):
        part.finish()


def second_kernel(nf, nt, width, v, op, hg, v_stage, op_stage, v_out, op_out, hg_out, op_later,
                  send, recv, z_send, z_recv, local):
    f, t = lax.axis_index("fsdp"), lax.axis_index("tensor")
    chip, core = f // 2, lax.rem(f, 2)
    greet(nf, nt)
    everyone = lambda to: (to, t)
    spread_v = Spread(
        nf, f, everyone, columns_of(v, width, width // 2 + width // 4, width // 4), v_stage, send.at[0], recv.at[0]
    )
    now, later = op_stage.shape[1], op_later.shape[1]
    spread_o = Spread(nf, f, everyone, lambda to: op.at[to, pl.ds(0, now)], op_stage, send.at[1], recv.at[1])
    spread_l = Spread(nf, f, everyone, lambda to: op.at[to, pl.ds(now, later)], op_later, send.at[3], recv.at[3])
    spread_h = Spread(
        nf // 2, chip, lambda to: (to * 2 + core, t), lambda to: hg.at[to], hg_out, send.at[2], recv.at[2]
    )
    along_v = Along(nf, nt, v_stage, v_out, z_send.at[0], z_recv.at[0], local.at[0])
    along_o = Along(nf, nt, op_stage, op_out, z_send.at[1], z_recv.at[1], local.at[1])
    spread_v.start()
    spread_o.start()
    along_v.start(spread_v.wait_for)
    along_o.start(spread_o.wait_for)
    spread_l.start()
    spread_h.start()
    for owner in range(nf):
        spread_l.wait_for(owner)
    for owner in range(nf // 2):
        spread_h.wait_for(owner)
    along_v.arrive()
    along_o.arrive()
    for part in (spread_v, spread_o, spread_l, spread_h, along_v, along_o):
        part.finish()


def step_kernel(scale, hid, cot, mask, w, m, va, vl, vb, new_w, new_m, new_v):
    f32 = jnp.float32
    blocks, _, width = cot.shape
    piece = width // 4
    corr_first = 1.0 - beta_first ** (STEP + 1)
    corr_second = 1.0 - beta_second ** (STEP + 1)
    for c in range(4):
        cols = slice(c * piece, (c + 1) * piece)
        total = None
        for n in range(blocks):
            part = lax.dot_general(
                hid[n], cot[n, :, cols], (((0,), (0,)), ((), ())), preferred_element_type=f32
            )
            part = (scale * part).astype(jnp.bfloat16).astype(f32)
            total = part if total is None else total + part
        kept = mask[:, cols] != 0
        grad = jnp.where(kept, total, 0.0)
        second = (va[...] if c == 0 else vb[...] if c == 3 else vl[:, (c - 1) * piece : c * piece]).astype(f32)
        weight = w[:, cols].astype(f32)
        first = beta_first * m[:, cols].astype(f32) + (1.0 - beta_first) * grad
        second = beta_second * second + (1.0 - beta_second) * grad * grad
        update = (first * (1.0 / corr_first)) / (jnp.sqrt(second * (1.0 / corr_second)) + epsilon)
        new_m[:, cols] = first
        new_v[:, cols] = second
        new_w[:, cols] = jnp.where(kept, weight - learn_rate * (update + decay_rate * weight), 0.0)


def body(saved_weight, saved_first, saved_second, saved_order, mask, hidden, cotangent):
    nf, nt = lax.axis_size("fsdp"), lax.axis_size("tensor")
    g = nf // nt
    band = saved_order.shape[0]
    width = saved_weight.shape[1] // nf
    tokens, rows = hidden.shape
    scale = (rows * nt) ** (-0.5)
    f32, bf16 = jnp.float32, jnp.bfloat16

    place = (saved_order[None, :] == jnp.arange(band, dtype=saved_order.dtype)[:, None]).astype(bf16)

    def arrange(saved):
        return jnp.dot(place, saved.astype(bf16), preferred_element_type=f32).astype(bf16)

    w, m, v = arrange(saved_weight), arrange(saved_first), arrange(saved_second)

    def shape(*dims):
        return jax.ShapeDtypeStruct(dims, bf16)

    def hop(stage):
        slots = stage.reshape((nt, g) + stage.shape[1:])
        pick = lambda j: lax.dynamic_index_in_dim(slots, lax.rem(t + j, nt), 0, keepdims=False)
        return [pick(0)] + [
            lax.ppermute(pick(j), "tensor", [(n, (n + j) % nt) for n in range(nt)]) for j in range(1, nt)
        ]

    def arranged(pieces):
        stacked = jnp.stack(pieces)
        return [
            lax.dynamic_index_in_dim(stacked, lax.rem(t - n + nt, nt), 0, keepdims=False) for n in range(nt)
        ]

    dma = pltpu.SemaphoreType.DMA
    t = lax.axis_index("tensor")
    half = width // 2
    stage, landed = shape(nf, band, width), shape(g, nt, band, width)
    stage_part, landed_part = shape(nf, band, width // 4), shape(g, nt, band, width // 4)
    keep = mask.astype(bf16)
    moved = pl.pallas_call(
        functools.partial(first_kernel, nf, nt, width),
        out_shape=(
            stage, stage, stage_part, landed, landed, landed_part, shape(nf, tokens, rows), shape(nf, tokens, width),
            landed, shape(nf // 2, tokens, width), shape(rows, width),
            shape(nf, band, half),
        ),
        in_specs=[ANY] * 6,
        out_specs=(ANY,) * 12,
        scratch_shapes=[
            dma((5, nf)), dma((5, nf)), dma((3, nt, g)), dma((3, nt, g)), dma((3, g)),
            dma((nf // 2,)), dma((nf // 2,)), dma((nf // 2,)), dma((nf // 2,)), dma((1,)),
            dma((nt, g)), dma((nt, g)), dma((nf // 2,)), dma((nf // 2,)), dma((1,)), dma((1,)),
        ],
        compiler_params=pltpu.CompilerParams(collective_id=0, has_side_effects=True),
        name="relay_weight",
    )(w, m, v, keep, hidden, cotangent)
    w_out, m_out, va_out, hid_all, cot_all, w_mate, cot_mate, keep_mate, v_later = moved[3:]
    vl_out = jnp.stack(arranged(hop(v_later)), axis=1)

    weight = w_out.reshape(rows, width)
    masked = weight * keep
    masked_mate = w_mate.reshape(rows, width) * keep_mate
    part_out = (scale * jnp.dot(hid_all.reshape(nf * tokens, rows), masked, preferred_element_type=f32)).astype(bf16)
    core = lax.rem(lax.axis_index("fsdp"), 2)
    cot_own = lax.dynamic_index_in_dim(cot_all.reshape(nf // 2, 2, tokens, width), core, 1, keepdims=False)

    def back(cot, masked):
        return lax.dot_general(
            cot.reshape(nf // 2 * tokens, width), masked, (((1,), (1,)), ((), ())), preferred_element_type=f32
        )

    part_grad = (scale * (back(cot_own, masked) + back(cot_mate, masked_mate))).astype(bf16)

    later = tokens * 3 // 8 // 16 * 16
    now = tokens - later
    moved = pl.pallas_call(
        functools.partial(second_kernel, nf, nt, width),
        out_shape=(
            shape(nf, band, width // 4), shape(nf, now, width), shape(g, nt, band, width // 4),
            shape(g, nt, now, width), shape(nf // 2, tokens, rows), shape(nf, later, width),
        ),
        in_specs=[ANY] * 3,
        out_specs=(ANY,) * 6,
        scratch_shapes=[
            dma((4, nf)), dma((4, nf)), dma((2, nt, g)), dma((2, nt, g)), dma((2, g)),
        ],
        compiler_params=pltpu.CompilerParams(collective_id=1, has_side_effects=True),
        name="relay_products",
    )(v, part_out.reshape(nf, tokens, width), part_grad.reshape(nf // 2, tokens, rows))
    vb_out, out_parts, grad_parts, out_later = moved[2:]
    out_later = hop(out_later)

    hidden_grad = jnp.sum(grad_parts.astype(f32), axis=0).astype(bf16)

    tile = 256 if rows % 256 == 0 else 128
    whole = lambda cols: pl.BlockSpec((tile, cols), lambda r: (r, 0))
    result = jax.ShapeDtypeStruct((rows, width), f32)
    new_weight, new_first, new_second = pl.pallas_call(
        functools.partial(step_kernel, scale),
        grid=(rows // tile,),
        out_shape=(result,) * 3,
        in_specs=[
            pl.BlockSpec((nf, tokens, tile), lambda r: (0, 0, r)),
            pl.BlockSpec((nf, tokens, width), lambda r: (0, 0, 0)),
            whole(width), whole(width), whole(width), whole(width // 4), whole(half), whole(width // 4),
        ],
        out_specs=(whole(width),) * 3,
        compiler_params=pltpu.CompilerParams(vmem_limit_bytes=48 * 2**20),
        cost_estimate=pl.CostEstimate(
            flops=2 * nf * tokens * rows * width, bytes_accessed=50 * rows * width // 2, transcendentals=rows * width
        ),
        name="grad_and_step",
    )(
        hid_all, cot_all, mask, weight, m_out.reshape(rows, width),
        va_out.reshape(rows, width // 4), vl_out.reshape(rows, half), vb_out.reshape(rows, width // 4),
    )
    output = jnp.concatenate(
        [jnp.sum(out_parts.astype(f32), axis=1), sum(piece.astype(f32) for piece in out_later)], axis=1
    ).astype(bf16)
    output = output.transpose(1, 0, 2).reshape(tokens, g * width)
    return (output, hidden_grad, new_weight, new_first, new_second)


def solution(mesh):
    return jax.shard_map(
        body,
        mesh=mesh,
        in_specs=(
            P(("fsdp", "tensor"), None),
            P(("fsdp", "tensor"), None),
            P(("fsdp", "tensor"), None),
            P(("fsdp", "tensor")),
            P("tensor", "fsdp"),
            P("fsdp", "tensor"),
            P("fsdp", None),
        ),
        out_specs=(
            P("fsdp", "tensor"),
            P("fsdp", "tensor"),
            P("tensor", "fsdp"),
            P("tensor", "fsdp"),
            P("tensor", "fsdp"),
        ),
        check_vma=False,
    )
```
